32 devices in a mesh: dp: 2 (over y), expert: 16 (over z, x, core).
Axes of the slice: x: 2, y: 2, z: 4, core: 2. Of those that a mesh axis runs over, the one named last changes fastest.
Arguments:
- tokens: bfloat16 [2, 512, 3584], P(None, ('dp', 'expert')), may hold values from -6 to 6
- out_grad: bfloat16 [2, 512, 3584], P(None, ('dp', 'expert')), may hold values from -6 to 6
- expert_ids: int32 [2, 512, 4], P(None, ('dp', 'expert')), may hold values from 0 to 7, all different within a row
- route_probs: float32 [2, 512, 4], P(None, ('dp', 'expert')), may hold values from 0.1 to 0.6
- copy_marks: int32 [2, 8], replicated, may hold values from 0 to 1, as said below
- w_gate: bfloat16 [3584, 8192], P(None, 'expert'), may hold values from -0.09375 to 0.09375
- w_up: bfloat16 [3584, 8192], P(None, 'expert'), may hold values from -0.09375 to 0.09375
- w_down: bfloat16 [3584, 8192], P(None, 'expert'), may hold values from -0.1875 to 0.1875
Outputs:
- moe_out: bfloat16 [2, 512, 3584], P(None, ('dp', 'expert'))
- input_grad: bfloat16 [2, 512, 3584], P(None, ('dp', 'expert'))
- grad_gate: float32 [3584, 8192], P('dp', 'expert')
- grad_up: float32 [3584, 8192], P('dp', 'expert')
- grad_down: float32 [3584, 8192], P('dp', 'expert')
The draws below stay inside these ranges and needn't reach their ends.
Inputs may be any that keep to these rules, and one draw needn't show every extreme that they name: `copy_marks`: each row has exactly 4 ones.
All inputs are finite; a program needn't handle non-finite values.
Results may differ from the reference program's by a relative error of at most 0.0064.
Values may be sent and summed in bfloat16 or wider, within the bound.
A program may use at most 128 MiB of HBM per device.

```python
import jax
import jax.numpy as jnp
from jax import lax

D = 3584
FF = 1024
SPLIT = 2
TOPK = 4
TOK_DEV = 16
FF_DEV = 512
EXPERTS = 8
HOT = 4
CAP = 8
TOKENS = 512
N_DP = 2
N_EXPERT = 16


def draw_copy_marks(key, part):
    rows = []
    for micro in range(2):
        order = jax.random.permutation(jax.random.fold_in(key, 11 + micro), EXPERTS)
        rows.append((order < HOT).astype(jnp.int32))
    return jnp.stack(rows)


def level_of(stream_key, extent, split, least, high):
    def one(axis_at, blocks):
        draws = jax.random.uniform(jax.random.fold_in(jax.random.fold_in(stream_key, 6), axis_at), (blocks,), jnp.float32, least / len(split), high / len(split))
        return jnp.repeat(jnp.exp(draws), extent[axis_at] // blocks).reshape((-1,) + (1,) * (len(extent) - axis_at - 1))

    level = one(*split[0])
    for cut in split[1:]:
        level = level * one(*cut)
    return level


def choose_distinct(stream_key, rows, number_of, top, lift):
    sequence = jax.random.permutation(jax.random.fold_in(stream_key, 1), number_of)
    favour = sequence
    for power in range(3):
        favour = favour * favour // number_of
    favour = favour * lift // number_of
    lots = jax.random.randint(jax.random.fold_in(stream_key, 2), (rows, number_of), 0, 4096) + favour
    fixed_rows = jax.random.permutation(jax.random.fold_in(stream_key, 3), rows)[jnp.arange(number_of) % rows]
    lots = jnp.where(jnp.arange(rows)[:, None] == fixed_rows[None, :], 1 << 14, lots)
    merit = lots * number_of + jnp.arange(number_of)
    return lax.top_k(merit.astype(jnp.int32), top)[1].astype(jnp.int32)


def scatter_about(rng, shape, deviation, limit, split=(), kind=jnp.bfloat16):
    level = level_of(rng, shape, split, -0.22, 0.18) if split else 1.0
    entries = jax.random.normal(rng, shape, jnp.float32) * deviation * level
    return jnp.minimum(jnp.maximum(entries, -limit), limit).astype(kind)


def setup_inputs(seed: int = 0) -> dict:
    arg_keys = jax.random.split(jax.random.key(seed), 9)
    tokens = scatter_about(arg_keys[0], (2, TOKENS, D), 1.0, 6.0, ((1, 32),))
    out_grad = scatter_about(arg_keys[1], (2, TOKENS, D), 1.0, 6.0, ((1, 32),))
    expert_ids = choose_distinct(arg_keys[2], 2 * TOKENS, EXPERTS, TOPK, 8192).reshape((2, TOKENS, TOPK))
    route_probs = jnp.clip(0.1 + 0.5 * jax.random.uniform(arg_keys[3], (2, TOKENS, TOPK), jnp.float32) ** level_of(arg_keys[3], (2, TOKENS, TOPK), ((1, 32),), -0.2, 0.2), 0.1, 0.6)
    copy_marks = draw_copy_marks(jax.random.fold_in(arg_keys[8], 71), 0)
    w_gate = scatter_about(arg_keys[5], (D, EXPERTS * FF), D ** -0.5, 0.09375, ((1, 16),))
    w_up = scatter_about(arg_keys[6], (D, EXPERTS * FF), D ** -0.5, 0.09375, ((1, 16),))
    w_down = scatter_about(arg_keys[7], (D, EXPERTS * FF), FF ** -0.5, 0.1875, ((1, 16),))
    return {"tokens": tokens, "out_grad": out_grad, "expert_ids": expert_ids, "route_probs": route_probs, "copy_marks": copy_marks, "w_gate": w_gate, "w_up": w_up, "w_down": w_down}


def expert_rows(rows_in, scaled, gate_w, up_w, down_w):
    contract = (((1,), (1,)), ((), ()))
    rows_first = (((0,), (0,)), ((), ()))
    gate_pre = jnp.dot(rows_in, gate_w, preferred_element_type=jnp.float32)
    up_pre = jnp.dot(rows_in, up_w, preferred_element_type=jnp.float32)
    squash = jax.nn.sigmoid(gate_pre)
    active = gate_pre * squash
    hidden = (active * up_pre).astype(jnp.bfloat16)
    part_out = lax.dot_general(hidden, down_w, contract, preferred_element_type=jnp.float32).astype(jnp.bfloat16)
    down_term = lax.dot_general(scaled, hidden, rows_first, preferred_element_type=jnp.float32)
    hidden_grad = jnp.dot(scaled, down_w, preferred_element_type=jnp.float32)
    gate_grad = (hidden_grad * up_pre * squash * (1.0 + gate_pre * (1.0 - squash))).astype(jnp.bfloat16)
    up_grad = (hidden_grad * active).astype(jnp.bfloat16)
    gate_term = lax.dot_general(rows_in, gate_grad, rows_first, preferred_element_type=jnp.float32)
    up_term = lax.dot_general(rows_in, up_grad, rows_first, preferred_element_type=jnp.float32)
    part_dx = lax.dot_general(gate_grad, gate_w, contract, preferred_element_type=jnp.float32)
    part_dx = (part_dx + lax.dot_general(up_grad, up_w, contract, preferred_element_type=jnp.float32)).astype(jnp.bfloat16)
    return part_out, part_dx, gate_term, up_term, down_term


def slot_tables(expert_ids, copy_marks):
    blocks = N_DP * N_EXPERT
    per_block = TOK_DEV * TOPK
    block_slots = 2 * CAP
    slots = blocks * block_slots
    total = blocks * per_block
    labels = jnp.arange(EXPERTS, dtype=jnp.int32)
    result = []
    for micro in range(2):
        flat = expert_ids[micro].reshape(blocks, per_block)
        onehot = (flat[:, :, None] == labels[None, None, :]).astype(jnp.int32)
        earlier = jnp.cumsum(onehot, axis=1) - onehot
        ranked = jnp.sum(earlier * onehot, axis=2)
        marked = jnp.sum(onehot * copy_marks[micro][None, None, :], axis=2)
        kept = (ranked < CAP) | ((marked > 0) & (ranked < 2 * CAP))
        starts = jnp.arange(blocks, dtype=jnp.int32)[:, None] * block_slots
        column = jnp.where(kept, starts + ranked, slots).reshape(total).astype(jnp.int32)
        owner = flat.reshape(total).astype(jnp.int32)
        table = jnp.full((EXPERTS, slots + 1), total, dtype=jnp.int32)
        table = table.at[owner, column].set(jnp.arange(total, dtype=jnp.int32))
        result.append(table[:, :slots])
    return jnp.stack(result)


def reference(tokens, out_grad, expert_ids, route_probs, copy_marks, w_gate, w_up, w_down):
    tables = slot_tables(expert_ids, copy_marks)
    total = TOKENS * TOPK
    slots = N_DP * N_EXPERT * 2 * CAP
    probs_flat = route_probs.reshape(2, total)

    def per_expert(carry, expert):
        moe_acc, grad_acc = carry
        start = expert * FF
        gate_w = lax.dynamic_slice_in_dim(w_gate, start, FF, 1)
        up_w = lax.dynamic_slice_in_dim(w_up, start, FF, 1)
        down_w = lax.dynamic_slice_in_dim(w_down, start, FF, 1)
        gate_sum = jnp.zeros((D, FF), jnp.float32)
        up_sum = jnp.zeros((D, FF), jnp.float32)
        down_sum = jnp.zeros((D, FF), jnp.float32)
        for micro in range(2):
            rows = tables[micro, expert]
            valid = rows < total
            safe = jnp.where(valid, rows, 0).astype(jnp.int32)
            token = (safe // TOPK).astype(jnp.int32)
            weight = jnp.where(valid, probs_flat[micro][safe], jnp.zeros((), jnp.float32))
            rows_in = jnp.where(valid[:, None], tokens[micro][token], jnp.zeros((), jnp.bfloat16))
            scaled = (weight[:, None] * out_grad[micro][token].astype(jnp.float32)).astype(jnp.bfloat16)
            out_sum = jnp.zeros((slots, D), jnp.float32)
            dx_sum = jnp.zeros((slots, D), jnp.float32)
            gate_parts = []
            up_parts = []
            down_parts = []
            for part in range(SPLIT):
                low = part * FF_DEV
                part_out, part_dx, gate_term, up_term, down_term = expert_rows(
                    rows_in, scaled, gate_w[:, low:low + FF_DEV], up_w[:, low:low + FF_DEV], down_w[:, low:low + FF_DEV])
                out_sum = out_sum + part_out.astype(jnp.float32)
                dx_sum = dx_sum + part_dx.astype(jnp.float32)
                gate_parts.append(gate_term)
                up_parts.append(up_term)
                down_parts.append(down_term)
            gate_sum = gate_sum + jnp.concatenate(gate_parts, axis=1)
            up_sum = up_sum + jnp.concatenate(up_parts, axis=1)
            down_sum = down_sum + jnp.concatenate(down_parts, axis=1)
            moe_acc = moe_acc.at[micro, token].add(weight[:, None] * out_sum)
            grad_acc = grad_acc.at[micro, token].add(jnp.where(valid[:, None], dx_sum, jnp.zeros((), jnp.float32)))
        return (moe_acc, grad_acc), (gate_sum, up_sum, down_sum)

    start_carry = (jnp.zeros((2, TOKENS, D), jnp.float32), jnp.zeros((2, TOKENS, D), jnp.float32))
    (moe_acc, grad_acc), grads = lax.scan(per_expert, start_carry, jnp.arange(EXPERTS, dtype=jnp.int32))

    def arrange(stacked):
        return jnp.moveaxis(stacked, 0, 1).reshape(D, EXPERTS * FF)

    return (moe_acc.astype(jnp.bfloat16), grad_acc.astype(jnp.bfloat16),
            arrange(grads[0]), arrange(grads[1]), arrange(grads[2]))
```

```python
import functools

import jax
import jax.numpy as jnp
from jax import lax
from jax.experimental import pallas as pl
from jax.experimental.pallas import tpu as pltpu
from jax.sharding import PartitionSpec as P

SPLIT = 2
CORES = 2
SIDES = 2
MESH = pl.DeviceIdType.MESH


def place(n_ep):
    me = lax.axis_index("expert")
    half = lax.axis_index("dp")
    core = lax.rem(me, CORES)
    side = lax.rem(lax.div(me, CORES), SIDES)
    layer = lax.div(me, CORES * SIDES)
    return half, layer, side, core


def block_of(layer, side, core):
    return (layer * SIDES + side) * CORES + core


def greet(layers, half, layer, side, core):
    barrier = pltpu.get_barrier_semaphore()
    peers = [(half, block_of(lax.rem(layer + k, layers), side, core)) for k in range(1, layers)]
    peers.append((half, block_of(layer, 1 - side, core)))
    peers.append((half, block_of(layer, side, 1 - core)))
    peers.append((1 - half, block_of(layer, side, core)))
    for peer in peers:
        pl.semaphore_signal(barrier, inc=1, device_id=peer, device_id_type=MESH)
    pl.semaphore_wait(barrier, len(peers))


def remote(src, dst, send, recv, peer):
    return pltpu.make_async_remote_copy(
        src_ref=src, dst_ref=dst, send_sem=send, recv_sem=recv, device_id=peer, device_id_type=MESH
    )


def gather_kernel(
    layers, t_ref, g_ref, w_ref, own_t, own_g, own_w, oth_t, oth_g,
    local_sem, zs, zr, xs, xr, cs, cr, ys, yr, fs, fr,
):
    half, layer, side, core = place(layers)
    me = block_of(layer, side, core)
    width = oth_t.shape[2]
    greet(layers, half, layer, side, core)
    own_in = (t_ref, g_ref, w_ref)
    own = (own_t, own_g, own_w)
    oth = (oth_t, oth_g)
    across = (half, block_of(layer, 1 - side, core))
    sibling = (half, block_of(layer, side, 1 - core))
    partner = (1 - half, me)
    cols = pl.ds(pl.multiple_of((1 - half) * width, 128), width)
    started = []

    def go(copy):
        copy.start()
        started.append(copy)
        return copy

    locals_ = []
    for a in range(3):
        copy = pltpu.make_async_copy(own_in[a], own[a].at[me], local_sem.at[a])
        copy.start()
        locals_.append(copy)
    z_in = {}
    for a in (2, 0, 1):
        for k in range(1, layers):
            peer = (half, block_of(lax.rem(layer + k, layers), side, core))
            z_in[a, k] = go(remote(own_in[a], own[a].at[me], zs.at[a, k], zr.at[a, k], peer))

    def hand_on(a, src, b, k, slot_x):
        if slot_x is not None:
            go(remote(src, own[a].at[b], xs.at[a, slot_x], xr.at[a, slot_x], across))
        if a < 2:
            part = src.at[:, cols]
            go(remote(part, oth[a].at[b], ys.at[a, k], yr.at[a, k], partner))
        go(remote(src, own[a].at[b], cs.at[a, k], cr.at[a, k], sibling))

    def from_side(k):
        b = block_of(lax.rem(layer - k + layers, layers), 1 - side, core)
        for a in (2, 0, 1):
            remote(own[a].at[b], own[a].at[b], xs.at[a, k], xr.at[a, k], across).wait_recv()
            hand_on(a, own[a].at[b], b, layers + k, None)

    for k in range(layers):
        b = block_of(lax.rem(layer - k + layers, layers), side, core)
        for a in (2, 0, 1):
            if k > 0:
                z_in[a, k].wait_recv()
            src = own_in[a] if k == 0 else own[a].at[b]
            hand_on(a, src, b, k, k)
        if k > 0:
            from_side(k - 1)
    from_side(layers - 1)

    def source(k, c):
        s = side if k < layers else 1 - side
        return block_of(lax.rem(layer - k % layers + layers, layers), s, c)

    for k in range(2 * layers):
        b = source(k, core)
        for a in range(2):
            dst = oth[a].at[b]
            remote(dst, dst, ys.at[a, k], yr.at[a, k], partner).wait_recv()
            go(remote(dst, dst, fs.at[a, k], fr.at[a, k], sibling))
    for k in range(2 * layers):
        b = source(k, 1 - core)
        for a in range(3):
            dst = own[a].at[b]
            remote(dst, dst, cs.at[a, k], cr.at[a, k], sibling).wait_recv()
        for a in range(2):
            dst = oth[a].at[b]
            remote(dst, dst, fs.at[a, k], fr.at[a, k], sibling).wait_recv()
    for copy in locals_:
        copy.wait()
    for copy in started:
        copy.wait_send()


def gather(layers, tokens, cots, weights):
    rows, width = tokens.shape
    blocks = layers * SIDES * CORES
    dma = pltpu.SemaphoreType.DMA
    anywhere = pl.BlockSpec(memory_space=pl.ANY)
    moved = blocks * rows * width * 6
    return pl.pallas_call(
        functools.partial(gather_kernel, layers),
        out_shape=(
            jax.ShapeDtypeStruct((blocks, rows, width), tokens.dtype),
            jax.ShapeDtypeStruct((blocks, rows, width), cots.dtype),
            jax.ShapeDtypeStruct((blocks, rows, weights.shape[1]), weights.dtype),
            jax.ShapeDtypeStruct((blocks, rows, width // 2), tokens.dtype),
            jax.ShapeDtypeStruct((blocks, rows, width // 2), cots.dtype),
        ),
        in_specs=[anywhere] * 3,
        out_specs=(anywhere,) * 5,
        scratch_shapes=[
            dma((3,)),
            dma((3, layers)), dma((3, layers)),
            dma((3, layers)), dma((3, layers)),
            dma((3, 2 * layers)), dma((3, 2 * layers)),
            dma((2, 2 * layers)), dma((2, 2 * layers)),
            dma((2, 2 * layers)), dma((2, 2 * layers)),
        ],
        compiler_params=pltpu.CompilerParams(collective_id=0, has_side_effects=True),
        cost_estimate=pl.CostEstimate(flops=0, bytes_accessed=moved, transcendentals=0),
        name="gather_rows",
    )(tokens, cots, weights)


def return_kernel(
    layers, r0, r1, acts, out0, out1, oth_acts, mine, from_core, from_side, from_layer,
    local_sem, cs, cr, xs, xr, zs, zr, hs, hr,
):
    half, layer, side, core = place(layers)
    greet(layers, half, layer, side, core)
    width = out0.shape[1]
    step = next(s for s in (512, 256, 128) if width % s == 0)
    across = (half, block_of(layer, 1 - side, core))
    sibling = (half, block_of(layer, side, 1 - core))
    partner = (1 - half, block_of(layer, side, core))
    parts = (r0, r1)
    outs = (out0, out1)
    swap = remote(acts, oth_acts, hs, hr, partner)
    swap.start()
    core_in = {}
    local_in = {}
    for k in range(layers):
        goal = lax.rem(layer + 1 + k, layers)
        for j in range(2):
            s = 1 - side if j == 0 else side
            i = 2 * k + j
            for a in range(2):
                core_in[a, i] = remote(
                    parts[a].at[block_of(goal, s, 1 - core)], from_core.at[a, i], cs.at[a, i], cr.at[a, i], sibling
                )
                core_in[a, i].start()
                local_in[a, i] = pltpu.make_async_copy(
                    parts[a].at[block_of(goal, s, core)], mine.at[a, i], local_sem.at[a, i]
                )
                local_in[a, i].start()
    side_in = {}
    layer_in = {}

    def chunks(body):
        @pl.loop(0, width // step)
        def _(q):
            body(pl.ds(pl.multiple_of(q * step, step), step))

    f32 = jnp.float32

    def first(k):
        i = 2 * k
        for a in range(2):
            local_in[a, i].wait()
            core_in[a, i].wait_recv()

            def body(c):
                total = mine[a, i, :, c].astype(f32) + from_core[a, i, :, c].astype(f32)
                mine[a, i, :, c] = total.astype(mine.dtype)

            chunks(body)
            side_in[a, k] = remote(mine.at[a, i], from_side.at[a, k], xs.at[a, k], xr.at[a, k], across)
            side_in[a, k].start()

    def second(k):
        i = 2 * k + 1
        for a in range(2):
            local_in[a, i].wait()
            core_in[a, i].wait_recv()
            side_in[a, k].wait_recv()
            if k < layers - 1:

                def body(c):
                    total = mine[a, i, :, c].astype(f32) + from_core[a, i, :, c].astype(f32)
                    total = total + from_side[a, k, :, c].astype(f32)
                    mine[a, i, :, c] = total.astype(mine.dtype)

                chunks(body)
                goal = lax.rem(layer + 1 + k, layers)
                layer_in[a, k] = remote(
                    mine.at[a, i], from_layer.at[a, k], zs.at[a, k], zr.at[a, k], (half, block_of(goal, side, core))
                )
                layer_in[a, k].start()

    first(0)
    for k in range(layers):
        if k + 1 < layers:
            first(k + 1)
        second(k)
    for a in range(2):
        for k in range(layers - 1):
            layer_in[a, k].wait_recv()
        i = 2 * layers - 1

        def body(c):
            total = mine[a, i, :, c].astype(f32) + from_core[a, i, :, c].astype(f32)
            total = total + from_side[a, layers - 1, :, c].astype(f32)
            for k in range(layers - 1):
                total = total + from_layer[a, k, :, c].astype(f32)
            outs[a][:, c] = total.astype(outs[a].dtype)

        chunks(body)
    swap.wait()
    for copies in (core_in, side_in, layer_in):
        for copy in copies.values():
            copy.wait_send()


def give_back(layers, part_out, part_dx, acts):
    blocks, rows, width = part_out.shape
    dma = pltpu.SemaphoreType.DMA
    anywhere = pl.BlockSpec(memory_space=pl.ANY)
    whole = pl.BlockSpec(memory_space=pltpu.VMEM)
    kind = part_out.dtype
    need = rows * width * 2 * 2 * (2 * 2 * layers + layers + layers + 2)
    return pl.pallas_call(
        functools.partial(return_kernel, layers),
        out_shape=(
            jax.ShapeDtypeStruct((rows, width), kind),
            jax.ShapeDtypeStruct((rows, width), kind),
            jax.ShapeDtypeStruct(acts.shape, acts.dtype),
        ),
        in_specs=[anywhere] * 3,
        out_specs=(whole, whole, anywhere),
        scratch_shapes=[
            pltpu.VMEM((2, 2 * layers, rows, width), kind),
            pltpu.VMEM((2, 2 * layers, rows, width), kind),
            pltpu.VMEM((2, layers, rows, width), kind),
            pltpu.VMEM((2, layers - 1, rows, width), kind),
            dma((2, 2 * layers)),
            dma((2, 2 * layers)), dma((2, 2 * layers)),
            dma((2, layers)), dma((2, layers)),
            dma((2, layers - 1)), dma((2, layers - 1)),
            dma, dma,
        ],
        compiler_params=pltpu.CompilerParams(
            collective_id=1, has_side_effects=True, vmem_limit_bytes=min(need + (4 << 20), 60 << 20)
        ),
        cost_estimate=pl.CostEstimate(flops=0, bytes_accessed=need, transcendentals=0),
        name="return_rows",
    )(part_out, part_dx, acts)


def dense_weights(expert_ids, probs, marks, experts, capacity):
    tok_rows = expert_ids.shape[1]
    labels = jnp.arange(experts, dtype=jnp.int32)
    onehot = expert_ids[:, :, :, None] == labels
    chosen = jnp.any(onehot, axis=2)
    weight = jnp.sum(jnp.where(onehot, probs[:, :, :, None], 0.0), axis=2)
    at = jnp.arange(tok_rows, dtype=jnp.int32)
    before = at[None, :, None, None] > at[None, None, :, None]
    ranked = jnp.sum((before & chosen[:, None, :, :]).astype(jnp.int32), axis=2)
    limit = jnp.where(marks[:, None, :] > 0, 2 * capacity, capacity)
    return jnp.where(chosen & (ranked < limit), weight, 0.0)


def local(tokens, out_grad, expert_ids, route_probs, copy_marks, w_gate, w_up, w_down):
    n_ep = lax.axis_size("expert")
    experts = n_ep // SPLIT
    layers = n_ep // (SIDES * CORES)
    tok_rows, topk = (expert_ids.shape[1], expert_ids.shape[2])
    width = tokens.shape[2]
    rows = 2 * tok_rows
    capacity = max(1, tok_rows * topk // experts)
    half = lax.axis_index("dp")
    expert = lax.axis_index("expert") // SPLIT
    f32 = jnp.float32
    bf16 = jnp.bfloat16
    weights = dense_weights(expert_ids, route_probs, copy_marks, experts, capacity).reshape(rows, experts)
    lanes = -(-experts // 128) * 128
    weights = jnp.pad(weights, ((0, 0), (0, lanes - experts)))
    own_t, own_g, own_w, oth_t, oth_g = gather(
        layers, tokens.reshape(rows, width), out_grad.reshape(rows, width), weights
    )
    own_t = own_t.reshape(-1, width)
    own_g = own_g.reshape(-1, width)
    oth_t = oth_t.reshape(-1, width // 2)
    oth_g = oth_g.reshape(-1, width // 2)
    mine = jnp.arange(lanes, dtype=jnp.int32) == expert
    p = jnp.sum(jnp.where(mine, own_w.reshape(-1, lanes), 0.0), axis=1, keepdims=True)
    contract = (((1,), (1,)), ((), ()))
    rows_first = (((0,), (0,)), ((), ()))
    gate_pre = jnp.dot(own_t, w_gate, preferred_element_type=f32)
    up_pre = jnp.dot(own_t, w_up, preferred_element_type=f32)
    squash = jax.nn.sigmoid(gate_pre)
    active = gate_pre * squash
    hidden = (p * (active * up_pre)).astype(bf16)
    hidden_grad = p * jnp.dot(own_g, w_down, preferred_element_type=f32)
    gate_grad = (hidden_grad * up_pre * squash * (1.0 + gate_pre * (1.0 - squash))).astype(bf16)
    up_grad = (hidden_grad * active).astype(bf16)
    part_out = lax.dot_general(hidden, w_down, contract, preferred_element_type=f32).astype(bf16)
    part_dx = lax.dot_general(gate_grad, w_gate, contract, preferred_element_type=f32)
    part_dx = (part_dx + lax.dot_general(up_grad, w_up, contract, preferred_element_type=f32)).astype(bf16)
    acts = jnp.stack([gate_grad, up_grad, hidden])
    moe, grad_in, oth_acts = give_back(
        layers, part_out.reshape(-1, rows, width), part_dx.reshape(-1, rows, width), acts
    )
    my_t = lax.dynamic_slice_in_dim(own_t, half * (width // 2), width // 2, 1)
    my_g = lax.dynamic_slice_in_dim(own_g, half * (width // 2), width // 2, 1)

    def outer(near, near_act, far, far_act):
        total = lax.dot_general(near, near_act, rows_first, preferred_element_type=f32)
        return total + lax.dot_general(far, far_act, rows_first, preferred_element_type=f32)

    return (
        moe.reshape(tokens.shape),
        grad_in.reshape(tokens.shape),
        outer(my_t, gate_grad, oth_t, oth_acts[0]),
        outer(my_t, up_grad, oth_t, oth_acts[1]),
        outer(my_g, hidden, oth_g, oth_acts[2]),
    )


def solution(mesh):
    return jax.shard_map(
        local,
        mesh=mesh,
        in_specs=(
            P(None, ("dp", "expert"), None),
            P(None, ("dp", "expert"), None),
            P(None, ("dp", "expert"), None),
            P(None, ("dp", "expert"), None),
            P(),
            P(None, "expert"),
            P(None, "expert"),
            P(None, "expert"),
        ),
        out_specs=(
            P(None, ("dp", "expert"), None),
            P(None, ("dp", "expert"), None),
            P("dp", "expert"),
            P("dp", "expert"),
            P("dp", "expert"),
        ),
        check_vma=False,
    )
```

```python
import functools

import jax
import jax.numpy as jnp
from jax import lax
from jax.experimental import pallas as pl
from jax.experimental.pallas import tpu as pltpu
from jax.sharding import PartitionSpec as P

SPLIT = 2
CORES = 2
SIDES = 2
MESH = pl.DeviceIdType.MESH


def place(n_ep):
    me = lax.axis_index("expert")
    half = lax.axis_index("dp")
    core = lax.rem(me, CORES)
    side = lax.rem(lax.div(me, CORES), SIDES)
    layer = lax.div(me, CORES * SIDES)
    return half, layer, side, core


def block_of(layer, side, core):
    return (layer * SIDES + side) * CORES + core


def greet(layers, half, layer, side, core):
    barrier = pltpu.get_barrier_semaphore()
    peers = [(half, block_of(lax.rem(layer + k, layers), side, core)) for k in range(1, layers)]
    peers.append((half, block_of(layer, 1 - side, core)))
    peers.append((half, block_of(layer, side, 1 - core)))
    peers.append((1 - half, block_of(layer, side, core)))
    for peer in peers:
        pl.semaphore_signal(barrier, inc=1, device_id=peer, device_id_type=MESH)
    pl.semaphore_wait(barrier, len(peers))


def remote(src, dst, send, recv, peer):
    return pltpu.make_async_remote_copy(
        src_ref=src, dst_ref=dst, send_sem=send, recv_sem=recv, device_id=peer, device_id_type=MESH
    )


def gather_kernel(
    layers, t_ref, g_ref, w_ref, own_t, own_g, own_w, oth_t, oth_g,
    local_sem, zs, zr, xs, xr, cs, cr, ys, yr, fs, fr,
):
    half, layer, side, core = place(layers)
    me = block_of(layer, side, core)
    width = oth_t.shape[2]
    greet(layers, half, layer, side, core)
    own_in = (t_ref, g_ref, w_ref)
    own = (own_t, own_g, own_w)
    oth = (oth_t, oth_g)
    across = (half, block_of(layer, 1 - side, core))
    sibling = (half, block_of(layer, side, 1 - core))
    partner = (1 - half, me)
    cols = pl.ds(pl.multiple_of((1 - half) * width, 128), width)
    slots = 2 * layers - 1
    arrays = (2, 0, 1)

    def reach(n):
        if n == 0:
            return True, layer
        if n < layers:
            return layer >= n, layer - n
        return layer + (n - layers + 1) < layers, layer + (n - layers + 1)

    def given(condition, body):
        if condition is True:
            body()
        else:
            pl.when(condition)(body)

    def along_copy(a, src, b, up, step):
        n = step if up else layers - 1 + step
        there = layer + 1 if up else layer - 1
        return remote(src, own[a].at[b], zs.at[a, n], zr.at[a, n], (half, block_of(there, side, core)))

    def copies(a, src, b, n, through):
        found = []
        if not through:
            found.append(remote(src, own[a].at[b], xs.at[a, n], xr.at[a, n], across))
        m = n + slots if through else n
        if a < 2:
            found.append(remote(src.at[:, cols], oth[a].at[b], ys.at[a, m], yr.at[a, m], partner))
        found.append(remote(src, own[a].at[b], cs.at[a, m], cr.at[a, m], sibling))
        return found

    locals_ = []
    for a in range(3):
        copy = pltpu.make_async_copy(own_in[a], own[a].at[me], local_sem.at[a])
        copy.start()
        locals_.append(copy)

    def at_start():
        for a in arrays:
            for up in (True, False):
                ok = layer + 1 < layers if up else layer > 0
                pl.when(ok)(lambda a=a, up=up: along_copy(a, own_in[a], me, up, 1).start())
            for copy in copies(a, own_in[a], me, 0, False):
                copy.start()

    def arrived(n):
        ok, origin = reach(n)
        up = n < layers
        step = n if up else n - layers + 1

        def body():
            b = block_of(origin, side, core)
            for a in arrays:
                dst = own[a].at[b]
                remote(dst, dst, zs.at[a, n], zr.at[a, n], sibling).wait_recv()
                if step + 1 < layers:
                    more = layer + 1 < layers if up else layer > 0
                    pl.when(more)(lambda a=a, dst=dst: along_copy(a, dst, b, up, step + 1).start())
                for copy in copies(a, dst, b, n, False):
                    copy.start()

        given(ok, body)

    def from_side(n):
        ok, origin = reach(n)

        def body():
            b = block_of(origin, 1 - side, core)
            for a in arrays:
                dst = own[a].at[b]
                remote(dst, dst, xs.at[a, n], xr.at[a, n], across).wait_recv()
                for copy in copies(a, dst, b, n, True):
                    copy.start()

        given(ok, body)

    at_start()
    for step in range(1, layers):
        arrived(step)
        arrived(layers - 1 + step)
        if step == 1:
            from_side(0)
        else:
            from_side(step - 1)
            from_side(layers + step - 2)
    from_side(layers - 1)
    from_side(2 * layers - 2)

    def each(body):
        for through in (False, True):
            for n in range(slots):
                ok, origin = reach(n)
                m = n + slots if through else n
                s = 1 - side if through else side
                given(ok, lambda n=n, m=m, s=s, origin=origin, through=through: body(n, m, s, origin, through))

    def pass_on(n, m, s, origin, through):
        b = block_of(origin, s, core)
        for a in range(2):
            dst = oth[a].at[b]
            remote(dst, dst, ys.at[a, m], yr.at[a, m], partner).wait_recv()
            remote(dst, dst, fs.at[a, m], fr.at[a, m], sibling).start()

    def finish(n, m, s, origin, through):
        b = block_of(origin, s, 1 - core)
        for a in range(3):
            dst = own[a].at[b]
            remote(dst, dst, cs.at[a, m], cr.at[a, m], sibling).wait_recv()
            if a < 2:
                dst = oth[a].at[b]
                remote(dst, dst, fs.at[a, m], fr.at[a, m], sibling).wait_recv()
        mine = block_of(origin, s, core)
        for a in range(3):
            for copy in copies(a, own[a].at[mine], mine, n, through):
                copy.wait_send()
            if a < 2:
                dst = oth[a].at[mine]
                remote(dst, dst, fs.at[a, m], fr.at[a, m], sibling).wait_send()
            if not through:
                step_up = n + 1 if n < layers else None
                step_dn = 1 if n == 0 else (n - layers + 2 if n >= layers else None)
                for up, step in ((True, step_up), (False, step_dn)):
                    if step is not None and step < layers:
                        more = layer + 1 < layers if up else layer > 0
                        pl.when(more)(
                            lambda a=a, up=up, step=step: along_copy(a, own[a].at[mine], mine, up, step).wait_send()
                        )

    each(pass_on)
    each(finish)
    for copy in locals_:
        copy.wait()


def gather(layers, tokens, cots, weights):
    rows, width = tokens.shape
    blocks = layers * SIDES * CORES
    dma = pltpu.SemaphoreType.DMA
    anywhere = pl.BlockSpec(memory_space=pl.ANY)
    moved = blocks * rows * width * 6
    slots = 2 * layers - 1
    return pl.pallas_call(
        functools.partial(gather_kernel, layers),
        out_shape=(
            jax.ShapeDtypeStruct((blocks, rows, width), tokens.dtype),
            jax.ShapeDtypeStruct((blocks, rows, width), cots.dtype),
            jax.ShapeDtypeStruct((blocks, rows, weights.shape[1]), weights.dtype),
            jax.ShapeDtypeStruct((blocks, rows, width // 2), tokens.dtype),
            jax.ShapeDtypeStruct((blocks, rows, width // 2), cots.dtype),
        ),
        in_specs=[anywhere] * 3,
        out_specs=(anywhere,) * 5,
        scratch_shapes=[
            dma((3,)),
            dma((3, slots)), dma((3, slots)),
            dma((3, slots)), dma((3, slots)),
            dma((3, 2 * slots)), dma((3, 2 * slots)),
            dma((2, 2 * slots)), dma((2, 2 * slots)),
            dma((2, 2 * slots)), dma((2, 2 * slots)),
        ],
        compiler_params=pltpu.CompilerParams(collective_id=0, has_side_effects=True),
        cost_estimate=pl.CostEstimate(flops=0, bytes_accessed=moved, transcendentals=0),
        name="gather_rows",
    )(tokens, cots, weights)


def return_kernel(
    layers, r0, r1, acts, out0, out1, oth_acts, mine, from_core, from_side, from_layer,
    local_sem, cs, cr, xs, xr, zs, zr, hs, hr,
):
    half, layer, side, core = place(layers)
    greet(layers, half, layer, side, core)
    width = out0.shape[1]
    step = next(s for s in (512, 256, 128) if width % s == 0)
    across = (half, block_of(layer, 1 - side, core))
    sibling = (half, block_of(layer, side, 1 - core))
    partner = (1 - half, block_of(layer, side, core))
    parts = (r0, r1)
    outs = (out0, out1)
    swap = remote(acts, oth_acts, hs, hr, partner)
    swap.start()
    core_in = {}
    local_in = {}
    for k in range(layers):
        goal = lax.rem(layer + 1 + k, layers)
        for j in range(2):
            s = 1 - side if j == 0 else side
            i = 2 * k + j
            for a in range(2):
                core_in[a, i] = remote(
                    parts[a].at[block_of(goal, s, 1 - core)], from_core.at[a, i], cs.at[a, i], cr.at[a, i], sibling
                )
                core_in[a, i].start()
                local_in[a, i] = pltpu.make_async_copy(
                    parts[a].at[block_of(goal, s, core)], mine.at[a, i], local_sem.at[a, i]
                )
                local_in[a, i].start()
    side_in = {}
    layer_in = {}

    def chunks(body):
        @pl.loop(0, width // step)
        def _(q):
            body(pl.ds(pl.multiple_of(q * step, step), step))

    f32 = jnp.float32

    def first(k):
        i = 2 * k
        for a in range(2):
            local_in[a, i].wait()
            core_in[a, i].wait_recv()

            def body(c):
                total = mine[a, i, :, c].astype(f32) + from_core[a, i, :, c].astype(f32)
                mine[a, i, :, c] = total.astype(mine.dtype)

            chunks(body)
            side_in[a, k] = remote(mine.at[a, i], from_side.at[a, k], xs.at[a, k], xr.at[a, k], across)
            side_in[a, k].start()

    def second(k):
        i = 2 * k + 1
        for a in range(2):
            local_in[a, i].wait()
            core_in[a, i].wait_recv()
            side_in[a, k].wait_recv()
            if k < layers - 1:

                def body(c):
                    total = mine[a, i, :, c].astype(f32) + from_core[a, i, :, c].astype(f32)
                    total = total + from_side[a, k, :, c].astype(f32)
                    mine[a, i, :, c] = total.astype(mine.dtype)

                chunks(body)
                goal = lax.rem(layer + 1 + k, layers)
                layer_in[a, k] = remote(
                    mine.at[a, i], from_layer.at[a, k], zs.at[a, k], zr.at[a, k], (half, block_of(goal, side, core))
                )
                layer_in[a, k].start()

    first(0)
    for k in range(layers):
        if k + 1 < layers:
            first(k + 1)
        second(k)
    for a in range(2):
        for k in range(layers - 1):
            layer_in[a, k].wait_recv()
        i = 2 * layers - 1

        def body(c):
            total = mine[a, i, :, c].astype(f32) + from_core[a, i, :, c].astype(f32)
            total = total + from_side[a, layers - 1, :, c].astype(f32)
            for k in range(layers - 1):
                total = total + from_layer[a, k, :, c].astype(f32)
            outs[a][:, c] = total.astype(outs[a].dtype)

        chunks(body)
    swap.wait()
    for copies in (core_in, side_in, layer_in):
        for copy in copies.values():
            copy.wait_send()


def give_back(layers, part_out, part_dx, acts):
    blocks, rows, width = part_out.shape
    dma = pltpu.SemaphoreType.DMA
    anywhere = pl.BlockSpec(memory_space=pl.ANY)
    whole = pl.BlockSpec(memory_space=pltpu.VMEM)
    kind = part_out.dtype
    need = rows * width * 2 * 2 * (2 * 2 * layers + layers + layers + 2)
    return pl.pallas_call(
        functools.partial(return_kernel, layers),
        out_shape=(
            jax.ShapeDtypeStruct((rows, width), kind),
            jax.ShapeDtypeStruct((rows, width), kind),
            jax.ShapeDtypeStruct(acts.shape, acts.dtype),
        ),
        in_specs=[anywhere] * 3,
        out_specs=(whole, whole, anywhere),
        scratch_shapes=[
            pltpu.VMEM((2, 2 * layers, rows, width), kind),
            pltpu.VMEM((2, 2 * layers, rows, width), kind),
            pltpu.VMEM((2, layers, rows, width), kind),
            pltpu.VMEM((2, layers - 1, rows, width), kind),
            dma((2, 2 * layers)),
            dma((2, 2 * layers)), dma((2, 2 * layers)),
            dma((2, layers)), dma((2, layers)),
            dma((2, layers - 1)), dma((2, layers - 1)),
            dma, dma,
        ],
        compiler_params=pltpu.CompilerParams(
            collective_id=1, has_side_effects=True, vmem_limit_bytes=min(need + (4 << 20), 60 << 20)
        ),
        cost_estimate=pl.CostEstimate(flops=0, bytes_accessed=need, transcendentals=0),
        name="return_rows",
    )(part_out, part_dx, acts)


def dense_weights(expert_ids, probs, marks, experts, capacity):
    tok_rows = expert_ids.shape[1]
    labels = jnp.arange(experts, dtype=jnp.int32)
    onehot = expert_ids[:, :, :, None] == labels
    chosen = jnp.any(onehot, axis=2)
    weight = jnp.sum(jnp.where(onehot, probs[:, :, :, None], 0.0), axis=2)
    at = jnp.arange(tok_rows, dtype=jnp.int32)
    before = at[None, :, None, None] > at[None, None, :, None]
    ranked = jnp.sum((before & chosen[:, None, :, :]).astype(jnp.int32), axis=2)
    limit = jnp.where(marks[:, None, :] > 0, 2 * capacity, capacity)
    return jnp.where(chosen & (ranked < limit), weight, 0.0)


def local(tokens, out_grad, expert_ids, route_probs, copy_marks, w_gate, w_up, w_down):
    n_ep = lax.axis_size("expert")
    experts = n_ep // SPLIT
    layers = n_ep // (SIDES * CORES)
    tok_rows, topk = (expert_ids.shape[1], expert_ids.shape[2])
    width = tokens.shape[2]
    rows = 2 * tok_rows
    capacity = max(1, tok_rows * topk // experts)
    half = lax.axis_index("dp")
    expert = lax.axis_index("expert") // SPLIT
    f32 = jnp.float32
    bf16 = jnp.bfloat16
    weights = dense_weights(expert_ids, route_probs, copy_marks, experts, capacity).reshape(rows, experts)
    lanes = -(-experts // 128) * 128
    weights = jnp.pad(weights, ((0, 0), (0, lanes - experts)))
    own_t, own_g, own_w, oth_t, oth_g = gather(
        layers, tokens.reshape(rows, width), out_grad.reshape(rows, width), weights
    )
    own_t = own_t.reshape(-1, width)
    own_g = own_g.reshape(-1, width)
    oth_t = oth_t.reshape(-1, width // 2)
    oth_g = oth_g.reshape(-1, width // 2)
    mine = jnp.arange(lanes, dtype=jnp.int32) == expert
    p = jnp.sum(jnp.where(mine, own_w.reshape(-1, lanes), 0.0), axis=1, keepdims=True)
    contract = (((1,), (1,)), ((), ()))
    rows_first = (((0,), (0,)), ((), ()))
    gate_pre = jnp.dot(own_t, w_gate, preferred_element_type=f32)
    up_pre = jnp.dot(own_t, w_up, preferred_element_type=f32)
    squash = jax.nn.sigmoid(gate_pre)
    active = gate_pre * squash
    hidden = (p * (active * up_pre)).astype(bf16)
    hidden_grad = p * jnp.dot(own_g, w_down, preferred_element_type=f32)
    gate_grad = (hidden_grad * up_pre * squash * (1.0 + gate_pre * (1.0 - squash))).astype(bf16)
    up_grad = (hidden_grad * active).astype(bf16)
    part_out = lax.dot_general(hidden, w_down, contract, preferred_element_type=f32).astype(bf16)
    part_dx = lax.dot_general(gate_grad, w_gate, contract, preferred_element_type=f32)
    part_dx = (part_dx + lax.dot_general(up_grad, w_up, contract, preferred_element_type=f32)).astype(bf16)
    acts = jnp.stack([gate_grad, up_grad, hidden])
    moe, grad_in, oth_acts = give_back(
        layers, part_out.reshape(-1, rows, width), part_dx.reshape(-1, rows, width), acts
    )
    my_t = lax.dynamic_slice_in_dim(own_t, half * (width // 2), width // 2, 1)
    my_g = lax.dynamic_slice_in_dim(own_g, half * (width // 2), width // 2, 1)

    def outer(near, near_act, far, far_act):
        total = lax.dot_general(near, near_act, rows_first, preferred_element_type=f32)
        return total + lax.dot_general(far, far_act, rows_first, preferred_element_type=f32)

    return (
        moe.reshape(tokens.shape),
        grad_in.reshape(tokens.shape),
        outer(my_t, gate_grad, oth_t, oth_acts[0]),
        outer(my_t, up_grad, oth_t, oth_acts[1]),
        outer(my_g, hidden, oth_g, oth_acts[2]),
    )


def solution(mesh):
    return jax.shard_map(
        local,
        mesh=mesh,
        in_specs=(
            P(None, ("dp", "expert"), None),
            P(None, ("dp", "expert"), None),
            P(None, ("dp", "expert"), None),
            P(None, ("dp", "expert"), None),
            P(),
            P(None, "expert"),
            P(None, "expert"),
            P(None, "expert"),
        ),
        out_specs=(
            P(None, ("dp", "expert"), None),
            P(None, ("dp", "expert"), None),
            P("dp", "expert"),
            P("dp", "expert"),
            P("dp", "expert"),
        ),
        check_vma=False,
    )
```

```python
import functools

import jax
import jax.numpy as jnp
from jax import lax
from jax.experimental import pallas as pl
from jax.experimental.pallas import tpu as pltpu
from jax.sharding import PartitionSpec as P

SPLIT = 2
CORES = 2
SIDES = 2
MESH = pl.DeviceIdType.MESH


def place(n_ep):
    me = lax.axis_index("expert")
    half = lax.axis_index("dp")
    core = lax.rem(me, CORES)
    side = lax.rem(lax.div(me, CORES), SIDES)
    layer = lax.div(me, CORES * SIDES)
    return half, layer, side, core


def block_of(layer, side, core):
    return (layer * SIDES + side) * CORES + core


def greet(layers, half, layer, side, core):
    barrier = pltpu.get_barrier_semaphore()
    peers = [(half, block_of(lax.rem(layer + k, layers), side, core)) for k in range(1, layers)]
    peers.append((half, block_of(layer, 1 - side, core)))
    peers.append((half, block_of(layer, side, 1 - core)))
    peers.append((1 - half, block_of(layer, side, core)))
    for peer in peers:
        pl.semaphore_signal(barrier, inc=1, device_id=peer, device_id_type=MESH)
    pl.semaphore_wait(barrier, len(peers))


def remote(src, dst, send, recv, peer):
    return pltpu.make_async_remote_copy(
        src_ref=src, dst_ref=dst, send_sem=send, recv_sem=recv, device_id=peer, device_id_type=MESH
    )


def gather_kernel(
    layers, t_ref, g_ref, w_ref, own_t, own_g, own_w, oth_t, oth_g,
    local_sem, zs, zr, xs, xr, cs, cr, ys, yr, fs, fr,
):
    half, layer, side, core = place(layers)
    me = block_of(layer, side, core)
    width = oth_t.shape[2]
    greet(layers, half, layer, side, core)
    own_in = (t_ref, g_ref, w_ref)
    own = (own_t, own_g, own_w)
    oth = (oth_t, oth_g)
    across = (half, block_of(layer, 1 - side, core))
    sibling = (half, block_of(layer, side, 1 - core))
    partner = (1 - half, me)
    cols = pl.ds(pl.multiple_of((1 - half) * width, 128), width)
    slots = 2 * layers - 1
    arrays = (2, 0, 1)

    def reach(n):
        if n == 0:
            return True, layer
        if n < layers:
            return layer >= n, layer - n
        return layer + (n - layers + 1) < layers, layer + (n - layers + 1)

    def given(condition, body):
        if condition is True:
            body()
        else:
            pl.when(condition)(body)

    def along_copy(a, src, b, up, step):
        n = step if up else layers - 1 + step
        there = layer + 1 if up else layer - 1
        return remote(src, own[a].at[b], zs.at[a, n], zr.at[a, n], (half, block_of(there, side, core)))

    def copies(a, src, b, n, through):
        found = []
        if not through:
            found.append(remote(src, own[a].at[b], xs.at[a, n], xr.at[a, n], across))
        m = n + slots if through else n
        if a < 2:
            found.append(remote(src.at[:, cols], oth[a].at[b], ys.at[a, m], yr.at[a, m], partner))
        found.append(remote(src, own[a].at[b], cs.at[a, m], cr.at[a, m], sibling))
        return found

    locals_ = []
    for a in range(3):
        copy = pltpu.make_async_copy(own_in[a], own[a].at[me], local_sem.at[a])
        copy.start()
        locals_.append(copy)

    def at_start():
        for a in arrays:
            for up in (True, False):
                ok = layer + 1 < layers if up else layer > 0
                pl.when(ok)(lambda a=a, up=up: along_copy(a, own_in[a], me, up, 1).start())
            for copy in copies(a, own_in[a], me, 0, False):
                copy.start()

    def arrived(n):
        ok, origin = reach(n)
        up = n < layers
        step = n if up else n - layers + 1

        def body():
            b = block_of(origin, side, core)
            for a in arrays:
                dst = own[a].at[b]
                remote(dst, dst, zs.at[a, n], zr.at[a, n], sibling).wait_recv()
                if step + 1 < layers:
                    more = layer + 1 < layers if up else layer > 0
                    pl.when(more)(lambda a=a, dst=dst: along_copy(a, dst, b, up, step + 1).start())
                for copy in copies(a, dst, b, n, False):
                    copy.start()

        given(ok, body)

    def from_side(n):
        ok, origin = reach(n)

        def body():
            b = block_of(origin, 1 - side, core)
            for a in arrays:
                dst = own[a].at[b]
                remote(dst, dst, xs.at[a, n], xr.at[a, n], across).wait_recv()
                for copy in copies(a, dst, b, n, True):
                    copy.start()

        given(ok, body)

    at_start()
    for step in range(1, layers):
        arrived(step)
        arrived(layers - 1 + step)
        if step == 1:
            from_side(0)
        else:
            from_side(step - 1)
            from_side(layers + step - 2)
    from_side(layers - 1)
    from_side(2 * layers - 2)

    def each(body):
        for through in (False, True):
            for n in range(slots):
                ok, origin = reach(n)
                m = n + slots if through else n
                s = 1 - side if through else side
                given(ok, lambda n=n, m=m, s=s, origin=origin, through=through: body(n, m, s, origin, through))

    def pass_on(n, m, s, origin, through):
        b = block_of(origin, s, core)
        for a in range(2):
            dst = oth[a].at[b]
            remote(dst, dst, ys.at[a, m], yr.at[a, m], partner).wait_recv()
            remote(dst, dst, fs.at[a, m], fr.at[a, m], sibling).start()

    def finish(n, m, s, origin, through):
        b = block_of(origin, s, 1 - core)
        for a in range(3):
            dst = own[a].at[b]
            remote(dst, dst, cs.at[a, m], cr.at[a, m], sibling).wait_recv()
            if a < 2:
                dst = oth[a].at[b]
                remote(dst, dst, fs.at[a, m], fr.at[a, m], sibling).wait_recv()
        mine = block_of(origin, s, core)
        for a in range(3):
            for copy in copies(a, own[a].at[mine], mine, n, through):
                copy.wait_send()
            if a < 2:
                dst = oth[a].at[mine]
                remote(dst, dst, fs.at[a, m], fr.at[a, m], sibling).wait_send()
            if not through:
                step_up = n + 1 if n < layers else None
                step_dn = 1 if n == 0 else (n - layers + 2 if n >= layers else None)
                for up, step in ((True, step_up), (False, step_dn)):
                    if step is not None and step < layers:
                        more = layer + 1 < layers if up else layer > 0
                        pl.when(more)(
                            lambda a=a, up=up, step=step: along_copy(a, own[a].at[mine], mine, up, step).wait_send()
                        )

    each(pass_on)
    each(finish)
    for copy in locals_:
        copy.wait()


def gather(layers, tokens, cots, weights):
    rows, width = tokens.shape
    blocks = layers * SIDES * CORES
    dma = pltpu.SemaphoreType.DMA
    anywhere = pl.BlockSpec(memory_space=pl.ANY)
    moved = blocks * rows * width * 6
    slots = 2 * layers - 1
    return pl.pallas_call(
        functools.partial(gather_kernel, layers),
        out_shape=(
            jax.ShapeDtypeStruct((blocks, rows, width), tokens.dtype),
            jax.ShapeDtypeStruct((blocks, rows, width), cots.dtype),
            jax.ShapeDtypeStruct((blocks, rows, weights.shape[1]), weights.dtype),
            jax.ShapeDtypeStruct((blocks, rows, width // 2), tokens.dtype),
            jax.ShapeDtypeStruct((blocks, rows, width // 2), cots.dtype),
        ),
        in_specs=[anywhere] * 3,
        out_specs=(anywhere,) * 5,
        scratch_shapes=[
            dma((3,)),
            dma((3, slots)), dma((3, slots)),
            dma((3, slots)), dma((3, slots)),
            dma((3, 2 * slots)), dma((3, 2 * slots)),
            dma((2, 2 * slots)), dma((2, 2 * slots)),
            dma((2, 2 * slots)), dma((2, 2 * slots)),
        ],
        compiler_params=pltpu.CompilerParams(collective_id=0, has_side_effects=True),
        cost_estimate=pl.CostEstimate(flops=0, bytes_accessed=moved, transcendentals=0),
        name="gather_rows",
    )(tokens, cots, weights)


def return_kernel(
    layers, r0, r1, acts, out0, out1, oth_acts, mine, from_core, from_side, from_layer,
    local_sem, cs, cr, xs, xr, zs, zr, hs, hr,
):
    half, layer, side, core = place(layers)
    greet(layers, half, layer, side, core)
    width = out0.shape[1]
    step = next(s for s in (512, 256, 128) if width % s == 0)
    across = (half, block_of(layer, 1 - side, core))
    sibling = (half, block_of(layer, side, 1 - core))
    partner = (1 - half, block_of(layer, side, core))
    parts = (r0, r1)
    outs = (out0, out1)
    swap = remote(acts, oth_acts, hs, hr, partner)
    swap.start()
    core_in = {}
    local_in = {}
    for k in range(layers):
        goal = lax.rem(layer + 1 + k, layers)
        for j in range(2):
            s = 1 - side if j == 0 else side
            i = 2 * k + j
            for a in range(2):
                core_in[a, i] = remote(
                    parts[a].at[block_of(goal, s, 1 - core)], from_core.at[a, i], cs.at[a, i], cr.at[a, i], sibling
                )
                core_in[a, i].start()
                local_in[a, i] = pltpu.make_async_copy(
                    parts[a].at[block_of(goal, s, core)], mine.at[a, i], local_sem.at[a, i]
                )
                local_in[a, i].start()
    side_in = {}
    layer_in = {}

    def chunks(body):
        @pl.loop(0, width // step)
        def _(q):
            body(pl.ds(pl.multiple_of(q * step, step), step))

    f32 = jnp.float32

    units = [(k, a) for k in range(layers) for a in range(2)]

    def first(k, a):
        i = 2 * k
        local_in[a, i].wait()
        core_in[a, i].wait_recv()

        def body(c):
            total = mine[a, i, :, c].astype(f32) + from_core[a, i, :, c].astype(f32)
            mine[a, i, :, c] = total.astype(mine.dtype)

        chunks(body)
        side_in[a, k] = remote(mine.at[a, i], from_side.at[a, k], xs.at[a, k], xr.at[a, k], across)

    def second(k, a):
        i = 2 * k + 1
        local_in[a, i].wait()
        core_in[a, i].wait_recv()
        if k < layers - 1:

            def body(c):
                total = mine[a, i, :, c].astype(f32) + from_core[a, i, :, c].astype(f32)
                total = total + from_side[a, k, :, c].astype(f32)
                mine[a, i, :, c] = total.astype(mine.dtype)

            chunks(body)
            goal = lax.rem(layer + 1 + k, layers)
            layer_in[a, k] = remote(
                mine.at[a, i], from_layer.at[a, k], zs.at[a, k], zr.at[a, k], (half, block_of(goal, side, core))
            )
            layer_in[a, k].start()

    window = 2
    for k, a in units[:window]:
        first(k, a)
        side_in[a, k].start()
    for u, (k, a) in enumerate(units):
        later = units[u + window] if u + window < len(units) else None
        if later is not None:
            first(*later)
        side_in[a, k].wait_recv()
        if later is not None:
            side_in[later[1], later[0]].start()
        second(k, a)
    for a in range(2):
        for k in range(layers - 1):
            layer_in[a, k].wait_recv()
        i = 2 * layers - 1

        def body(c):
            total = mine[a, i, :, c].astype(f32) + from_core[a, i, :, c].astype(f32)
            total = total + from_side[a, layers - 1, :, c].astype(f32)
            for k in range(layers - 1):
                total = total + from_layer[a, k, :, c].astype(f32)
            outs[a][:, c] = total.astype(outs[a].dtype)

        chunks(body)
    swap.wait()
    for copies in (core_in, side_in, layer_in):
        for copy in copies.values():
            copy.wait_send()


def give_back(layers, part_out, part_dx, acts):
    blocks, rows, width = part_out.shape
    dma = pltpu.SemaphoreType.DMA
    anywhere = pl.BlockSpec(memory_space=pl.ANY)
    whole = pl.BlockSpec(memory_space=pltpu.VMEM)
    kind = part_out.dtype
    need = rows * width * 2 * 2 * (2 * 2 * layers + layers + layers + 2)
    return pl.pallas_call(
        functools.partial(return_kernel, layers),
        out_shape=(
            jax.ShapeDtypeStruct((rows, width), kind),
            jax.ShapeDtypeStruct((rows, width), kind),
            jax.ShapeDtypeStruct(acts.shape, acts.dtype),
        ),
        in_specs=[anywhere] * 3,
        out_specs=(whole, whole, anywhere),
        scratch_shapes=[
            pltpu.VMEM((2, 2 * layers, rows, width), kind),
            pltpu.VMEM((2, 2 * layers, rows, width), kind),
            pltpu.VMEM((2, layers, rows, width), kind),
            pltpu.VMEM((2, layers - 1, rows, width), kind),
            dma((2, 2 * layers)),
            dma((2, 2 * layers)), dma((2, 2 * layers)),
            dma((2, layers)), dma((2, layers)),
            dma((2, layers - 1)), dma((2, layers - 1)),
            dma, dma,
        ],
        compiler_params=pltpu.CompilerParams(
            collective_id=1, has_side_effects=True, vmem_limit_bytes=min(need + (4 << 20), 60 << 20)
        ),
        cost_estimate=pl.CostEstimate(flops=0, bytes_accessed=need, transcendentals=0),
        name="return_rows",
    )(part_out, part_dx, acts)


def dense_weights(expert_ids, probs, marks, experts, capacity):
    tok_rows = expert_ids.shape[1]
    labels = jnp.arange(experts, dtype=jnp.int32)
    onehot = expert_ids[:, :, :, None] == labels
    chosen = jnp.any(onehot, axis=2)
    weight = jnp.sum(jnp.where(onehot, probs[:, :, :, None], 0.0), axis=2)
    at = jnp.arange(tok_rows, dtype=jnp.int32)
    before = at[None, :, None, None] > at[None, None, :, None]
    ranked = jnp.sum((before & chosen[:, None, :, :]).astype(jnp.int32), axis=2)
    limit = jnp.where(marks[:, None, :] > 0, 2 * capacity, capacity)
    return jnp.where(chosen & (ranked < limit), weight, 0.0)


def local(tokens, out_grad, expert_ids, route_probs, copy_marks, w_gate, w_up, w_down):
    n_ep = lax.axis_size("expert")
    experts = n_ep // SPLIT
    layers = n_ep // (SIDES * CORES)
    tok_rows, topk = (expert_ids.shape[1], expert_ids.shape[2])
    width = tokens.shape[2]
    rows = 2 * tok_rows
    capacity = max(1, tok_rows * topk // experts)
    half = lax.axis_index("dp")
    expert = lax.axis_index("expert") // SPLIT
    f32 = jnp.float32
    bf16 = jnp.bfloat16
    weights = dense_weights(expert_ids, route_probs, copy_marks, experts, capacity).reshape(rows, experts)
    lanes = -(-experts // 128) * 128
    weights = jnp.pad(weights, ((0, 0), (0, lanes - experts)))
    own_t, own_g, own_w, oth_t, oth_g = gather(
        layers, tokens.reshape(rows, width), out_grad.reshape(rows, width), weights
    )
    own_t = own_t.reshape(-1, width)
    own_g = own_g.reshape(-1, width)
    oth_t = oth_t.reshape(-1, width // 2)
    oth_g = oth_g.reshape(-1, width // 2)
    mine = jnp.arange(lanes, dtype=jnp.int32) == expert
    p = jnp.sum(jnp.where(mine, own_w.reshape(-1, lanes), 0.0), axis=1, keepdims=True)
    contract = (((1,), (1,)), ((), ()))
    rows_first = (((0,), (0,)), ((), ()))
    gate_pre = jnp.dot(own_t, w_gate, preferred_element_type=f32)
    up_pre = jnp.dot(own_t, w_up, preferred_element_type=f32)
    squash = jax.nn.sigmoid(gate_pre)
    active = gate_pre * squash
    hidden = (p * (active * up_pre)).astype(bf16)
    hidden_grad = p * jnp.dot(own_g, w_down, preferred_element_type=f32)
    gate_grad = (hidden_grad * up_pre * squash * (1.0 + gate_pre * (1.0 - squash))).astype(bf16)
    up_grad = (hidden_grad * active).astype(bf16)
    part_out = lax.dot_general(hidden, w_down, contract, preferred_element_type=f32).astype(bf16)
    part_dx = lax.dot_general(gate_grad, w_gate, contract, preferred_element_type=f32)
    part_dx = (part_dx + lax.dot_general(up_grad, w_up, contract, preferred_element_type=f32)).astype(bf16)
    acts = jnp.stack([gate_grad, up_grad, hidden])
    moe, grad_in, oth_acts = give_back(
        layers, part_out.reshape(-1, rows, width), part_dx.reshape(-1, rows, width), acts
    )
    my_t = lax.dynamic_slice_in_dim(own_t, half * (width // 2), width // 2, 1)
    my_g = lax.dynamic_slice_in_dim(own_g, half * (width // 2), width // 2, 1)

    def outer(near, near_act, far, far_act):
        total = lax.dot_general(near, near_act, rows_first, preferred_element_type=f32)
        return total + lax.dot_general(far, far_act, rows_first, preferred_element_type=f32)

    return (
        moe.reshape(tokens.shape),
        grad_in.reshape(tokens.shape),
        outer(my_t, gate_grad, oth_t, oth_acts[0]),
        outer(my_t, up_grad, oth_t, oth_acts[1]),
        outer(my_g, hidden, oth_g, oth_acts[2]),
    )


def solution(mesh):
    return jax.shard_map(
        local,
        mesh=mesh,
        in_specs=(
            P(None, ("dp", "expert"), None),
            P(None, ("dp", "expert"), None),
            P(None, ("dp", "expert"), None),
            P(None, ("dp", "expert"), None),
            P(),
            P(None, "expert"),
            P(None, "expert"),
            P(None, "expert"),
        ),
        out_specs=(
            P(None, ("dp", "expert"), None),
            P(None, ("dp", "expert"), None),
            P("dp", "expert"),
            P("dp", "expert"),
            P("dp", "expert"),
        ),
        check_vma=False,
    )
```

```python
import functools

import jax
import jax.numpy as jnp
from jax import lax
from jax.experimental import pallas as pl
from jax.experimental.pallas import tpu as pltpu
from jax.sharding import PartitionSpec as P

SPLIT = 2
CORES = 2
SIDES = 2
MESH = pl.DeviceIdType.MESH


def place(n_ep):
    me = lax.axis_index("expert")
    half = lax.axis_index("dp")
    core = lax.rem(me, CORES)
    side = lax.rem(lax.div(me, CORES), SIDES)
    layer = lax.div(me, CORES * SIDES)
    return half, layer, side, core


def block_of(layer, side, core):
    return (layer * SIDES + side) * CORES + core


def greet(layers, half, layer, side, core):
    barrier = pltpu.get_barrier_semaphore()
    peers = [(half, block_of(lax.rem(layer + k, layers), side, core)) for k in range(1, layers)]
    peers.append((half, block_of(layer, 1 - side, core)))
    peers.append((half, block_of(layer, side, 1 - core)))
    peers.append((1 - half, block_of(layer, side, core)))
    for peer in peers:
        pl.semaphore_signal(barrier, inc=1, device_id=peer, device_id_type=MESH)
    pl.semaphore_wait(barrier, len(peers))


def remote(src, dst, send, recv, peer):
    return pltpu.make_async_remote_copy(
        src_ref=src, dst_ref=dst, send_sem=send, recv_sem=recv, device_id=peer, device_id_type=MESH
    )


def gather_kernel(
    layers, t_ref, g_ref, w_ref, own_t, own_g, own_w, oth_t, oth_g,
    local_sem, near_sem, zs, zr, xs, xr, cs, cr, ys, yr, fs, fr,
):
    half, layer, side, core = place(layers)
    me = block_of(layer, side, core)
    width = oth_t.shape[3]
    greet(layers, half, layer, side, core)
    own_in = (t_ref, g_ref, w_ref)
    own = (own_t, own_g, own_w)
    halves = (oth_t, oth_g)
    oth = (oth_t.at[1], oth_g.at[1])
    across = (half, block_of(layer, 1 - side, core))
    sibling = (half, block_of(layer, side, 1 - core))
    partner = (1 - half, me)
    cols = pl.ds(pl.multiple_of((1 - half) * width, 128), width)
    near = pl.ds(pl.multiple_of(half * width, 128), width)
    slots = 2 * layers - 1
    arrays = (2, 0, 1)

    def reach(n):
        if n == 0:
            return True, layer
        if n < layers:
            return layer >= n, layer - n
        return layer + (n - layers + 1) < layers, layer + (n - layers + 1)

    def given(condition, body):
        if condition is True:
            body()
        else:
            pl.when(condition)(body)

    def along_copy(a, src, b, up, step):
        n = step if up else layers - 1 + step
        there = layer + 1 if up else layer - 1
        return remote(src, own[a].at[b], zs.at[a, n], zr.at[a, n], (half, block_of(there, side, core)))

    def copies(a, src, b, n, through):
        found = []
        if not through:
            found.append(remote(src, own[a].at[b], xs.at[a, n], xr.at[a, n], across))
        m = n + slots if through else n
        if a < 2:
            found.append(remote(src.at[:, cols], oth[a].at[b], ys.at[a, m], yr.at[a, m], partner))
        found.append(remote(src, own[a].at[b], cs.at[a, m], cr.at[a, m], sibling))
        return found

    locals_ = []
    for a in range(3):
        copy = pltpu.make_async_copy(own_in[a], own[a].at[me], local_sem.at[a])
        copy.start()
        locals_.append(copy)

    def at_start():
        for a in arrays:
            for up in (True, False):
                ok = layer + 1 < layers if up else layer > 0
                pl.when(ok)(lambda a=a, up=up: along_copy(a, own_in[a], me, up, 1).start())
            for copy in copies(a, own_in[a], me, 0, False):
                copy.start()

    def arrived(n):
        ok, origin = reach(n)
        up = n < layers
        step = n if up else n - layers + 1

        def body():
            b = block_of(origin, side, core)
            for a in arrays:
                dst = own[a].at[b]
                remote(dst, dst, zs.at[a, n], zr.at[a, n], sibling).wait_recv()
                if step + 1 < layers:
                    more = layer + 1 < layers if up else layer > 0
                    pl.when(more)(lambda a=a, dst=dst: along_copy(a, dst, b, up, step + 1).start())
                for copy in copies(a, dst, b, n, False):
                    copy.start()

        given(ok, body)

    def from_side(n):
        ok, origin = reach(n)

        def body():
            b = block_of(origin, 1 - side, core)
            for a in arrays:
                dst = own[a].at[b]
                remote(dst, dst, xs.at[a, n], xr.at[a, n], across).wait_recv()
                for copy in copies(a, dst, b, n, True):
                    copy.start()

        given(ok, body)

    at_start()
    for step in range(1, layers):
        arrived(step)
        arrived(layers - 1 + step)
        if step == 1:
            from_side(0)
        else:
            from_side(step - 1)
            from_side(layers + step - 2)
    from_side(layers - 1)
    from_side(2 * layers - 2)

    def each(body):
        for through in (False, True):
            for n in range(slots):
                ok, origin = reach(n)
                m = n + slots if through else n
                s = 1 - side if through else side
                given(ok, lambda n=n, m=m, s=s, origin=origin, through=through: body(n, m, s, origin, through))

    def keep(a, b, m, first):
        src = own_in[a] if first else own[a].at[b]
        return pltpu.make_async_copy(src.at[:, near], halves[a].at[0, b], near_sem.at[a, m])

    def pass_on(n, m, s, origin, through):
        b = block_of(origin, s, core)
        for a in range(2):
            keep(a, b, m, n == 0 and not through).start()
            dst = oth[a].at[b]
            remote(dst, dst, ys.at[a, m], yr.at[a, m], partner).wait_recv()
            remote(dst, dst, fs.at[a, m], fr.at[a, m], sibling).start()

    def finish(n, m, s, origin, through):
        b = block_of(origin, s, 1 - core)
        for a in range(3):
            dst = own[a].at[b]
            remote(dst, dst, cs.at[a, m], cr.at[a, m], sibling).wait_recv()
            if a < 2:
                keep(a, b, m + 2 * slots, False).start()
                dst = oth[a].at[b]
                remote(dst, dst, fs.at[a, m], fr.at[a, m], sibling).wait_recv()
        mine = block_of(origin, s, core)
        for a in range(3):
            for copy in copies(a, own[a].at[mine], mine, n, through):
                copy.wait_send()
            if a < 2:
                dst = oth[a].at[mine]
                remote(dst, dst, fs.at[a, m], fr.at[a, m], sibling).wait_send()
            if not through:
                step_up = n + 1 if n < layers else None
                step_dn = 1 if n == 0 else (n - layers + 2 if n >= layers else None)
                for up, step in ((True, step_up), (False, step_dn)):
                    if step is not None and step < layers:
                        more = layer + 1 < layers if up else layer > 0
                        pl.when(more)(
                            lambda a=a, up=up, step=step: along_copy(a, own[a].at[mine], mine, up, step).wait_send()
                        )

    def settle(n, m, s, origin, through):
        for a in range(2):
            keep(a, block_of(origin, s, core), m, n == 0 and not through).wait()
            keep(a, block_of(origin, s, 1 - core), m + 2 * slots, False).wait()

    each(pass_on)
    each(finish)
    each(settle)
    for copy in locals_:
        copy.wait()


def gather(layers, tokens, cots, weights):
    rows, width = tokens.shape
    blocks = layers * SIDES * CORES
    dma = pltpu.SemaphoreType.DMA
    anywhere = pl.BlockSpec(memory_space=pl.ANY)
    moved = blocks * rows * width * 6
    slots = 2 * layers - 1
    return pl.pallas_call(
        functools.partial(gather_kernel, layers),
        out_shape=(
            jax.ShapeDtypeStruct((blocks, rows, width), tokens.dtype),
            jax.ShapeDtypeStruct((blocks, rows, width), cots.dtype),
            jax.ShapeDtypeStruct((blocks, rows, weights.shape[1]), weights.dtype),
            jax.ShapeDtypeStruct((2, blocks, rows, width // 2), tokens.dtype),
            jax.ShapeDtypeStruct((2, blocks, rows, width // 2), cots.dtype),
        ),
        in_specs=[anywhere] * 3,
        out_specs=(anywhere,) * 5,
        scratch_shapes=[
            dma((3,)),
            dma((2, 4 * slots)),
            dma((3, slots)), dma((3, slots)),
            dma((3, slots)), dma((3, slots)),
            dma((3, 2 * slots)), dma((3, 2 * slots)),
            dma((2, 2 * slots)), dma((2, 2 * slots)),
            dma((2, 2 * slots)), dma((2, 2 * slots)),
        ],
        compiler_params=pltpu.CompilerParams(collective_id=0, has_side_effects=True),
        cost_estimate=pl.CostEstimate(flops=0, bytes_accessed=moved, transcendentals=0),
        name="gather_rows",
    )(tokens, cots, weights)


def return_kernel(
    layers, r0, r1, a0, a1, a2, out0, out1, both0, both1, both2, mine, from_core, from_side, from_layer,
    local_sem, near_sem, cs, cr, xs, xr, zs, zr, hs, hr,
):
    half, layer, side, core = place(layers)
    greet(layers, half, layer, side, core)
    width = out0.shape[1]
    step = next(s for s in (512, 256, 128) if width % s == 0)
    across = (half, block_of(layer, 1 - side, core))
    sibling = (half, block_of(layer, side, 1 - core))
    partner = (1 - half, block_of(layer, side, core))
    parts = (r0, r1)
    outs = (out0, out1)
    acts = (a0, a1, a2)
    both = (both0, both1, both2)
    swaps = [remote(acts[n], both[n].at[1], hs.at[n], hr.at[n], partner) for n in range(3)]
    stays = [pltpu.make_async_copy(acts[n], both[n].at[0], near_sem.at[n]) for n in range(3)]
    core_in = {}
    local_in = {}
    for k in range(layers):
        goal = lax.rem(layer + 1 + k, layers)
        for j in range(2):
            s = 1 - side if j == 0 else side
            i = 2 * k + j
            for a in range(2):
                core_in[a, i] = remote(
                    parts[a].at[block_of(goal, s, 1 - core)], from_core.at[a, i], cs.at[a, i], cr.at[a, i], sibling
                )
                core_in[a, i].start()
                local_in[a, i] = pltpu.make_async_copy(
                    parts[a].at[block_of(goal, s, core)], mine.at[a, i], local_sem.at[a, i]
                )
                local_in[a, i].start()
    side_in = {}
    layer_in = {}

    def chunks(body):
        @pl.loop(0, width // step)
        def _(q):
            body(pl.ds(pl.multiple_of(q * step, step), step))

    f32 = jnp.float32

    units = [(k, a) for k in range(layers) for a in range(2)]

    def first(k, a):
        i = 2 * k
        local_in[a, i].wait()
        core_in[a, i].wait_recv()

        def body(c):
            total = mine[a, i, :, c].astype(f32) + from_core[a, i, :, c].astype(f32)
            mine[a, i, :, c] = total.astype(mine.dtype)

        chunks(body)
        side_in[a, k] = remote(mine.at[a, i], from_side.at[a, k], xs.at[a, k], xr.at[a, k], across)

    def second(k, a):
        i = 2 * k + 1
        local_in[a, i].wait()
        core_in[a, i].wait_recv()
        if k < layers - 1:

            def body(c):
                total = mine[a, i, :, c].astype(f32) + from_core[a, i, :, c].astype(f32)
                total = total + from_side[a, k, :, c].astype(f32)
                mine[a, i, :, c] = total.astype(mine.dtype)

            chunks(body)
            goal = lax.rem(layer + 1 + k, layers)
            layer_in[a, k] = remote(
                mine.at[a, i], from_layer.at[a, k], zs.at[a, k], zr.at[a, k], (half, block_of(goal, side, core))
            )
            layer_in[a, k].start()

    window = 2
    for k, a in units[:window]:
        first(k, a)
        side_in[a, k].start()
    for copy in swaps + stays:
        copy.start()
    for u, (k, a) in enumerate(units):
        later = units[u + window] if u + window < len(units) else None
        if later is not None:
            first(*later)
        side_in[a, k].wait_recv()
        if later is not None:
            side_in[later[1], later[0]].start()
        second(k, a)
    for a in range(2):
        for k in range(layers - 1):
            layer_in[a, k].wait_recv()
        i = 2 * layers - 1

        def body(c):
            total = mine[a, i, :, c].astype(f32) + from_core[a, i, :, c].astype(f32)
            total = total + from_side[a, layers - 1, :, c].astype(f32)
            for k in range(layers - 1):
                total = total + from_layer[a, k, :, c].astype(f32)
            outs[a][:, c] = total.astype(outs[a].dtype)

        chunks(body)
    for copy in swaps + stays:
        copy.wait()
    for copies in (core_in, side_in, layer_in):
        for copy in copies.values():
            copy.wait_send()


def give_back(layers, part_out, part_dx, acts):
    blocks, rows, width = part_out.shape
    dma = pltpu.SemaphoreType.DMA
    anywhere = pl.BlockSpec(memory_space=pl.ANY)
    whole = pl.BlockSpec(memory_space=pltpu.VMEM)
    kind = part_out.dtype
    need = rows * width * 2 * 2 * (2 * 2 * layers + layers + layers + 2)
    return pl.pallas_call(
        functools.partial(return_kernel, layers),
        out_shape=(
            jax.ShapeDtypeStruct((rows, width), kind),
            jax.ShapeDtypeStruct((rows, width), kind),
        ) + tuple(jax.ShapeDtypeStruct((2,) + act.shape, act.dtype) for act in acts),
        in_specs=[anywhere] * 5,
        out_specs=(whole, whole) + (anywhere,) * 3,
        scratch_shapes=[
            pltpu.VMEM((2, 2 * layers, rows, width), kind),
            pltpu.VMEM((2, 2 * layers, rows, width), kind),
            pltpu.VMEM((2, layers, rows, width), kind),
            pltpu.VMEM((2, layers - 1, rows, width), kind),
            dma((2, 2 * layers)),
            dma((3,)),
            dma((2, 2 * layers)), dma((2, 2 * layers)),
            dma((2, layers)), dma((2, layers)),
            dma((2, layers - 1)), dma((2, layers - 1)),
            dma((3,)), dma((3,)),
        ],
        compiler_params=pltpu.CompilerParams(
            collective_id=1, has_side_effects=True, vmem_limit_bytes=min(need + (4 << 20), 60 << 20)
        ),
        cost_estimate=pl.CostEstimate(flops=0, bytes_accessed=need, transcendentals=0),
        name="return_rows",
    )(part_out, part_dx, *acts)


def dense_weights(expert_ids, probs, marks, experts, capacity):
    tok_rows = expert_ids.shape[1]
    labels = jnp.arange(experts, dtype=jnp.int32)
    onehot = expert_ids[:, :, :, None] == labels
    chosen = jnp.any(onehot, axis=2)
    weight = jnp.sum(jnp.where(onehot, probs[:, :, :, None], 0.0), axis=2)
    at = jnp.arange(tok_rows, dtype=jnp.int32)
    before = at[None, :, None, None] > at[None, None, :, None]
    ranked = jnp.sum((before & chosen[:, None, :, :]).astype(jnp.int32), axis=2)
    limit = jnp.where(marks[:, None, :] > 0, 2 * capacity, capacity)
    return jnp.where(chosen & (ranked < limit), weight, 0.0)


def local(tokens, out_grad, expert_ids, route_probs, copy_marks, w_gate, w_up, w_down):
    n_ep = lax.axis_size("expert")
    experts = n_ep // SPLIT
    layers = n_ep // (SIDES * CORES)
    tok_rows, topk = (expert_ids.shape[1], expert_ids.shape[2])
    width = tokens.shape[2]
    rows = 2 * tok_rows
    capacity = max(1, tok_rows * topk // experts)
    expert = lax.axis_index("expert") // SPLIT
    f32 = jnp.float32
    bf16 = jnp.bfloat16
    weights = dense_weights(expert_ids, route_probs, copy_marks, experts, capacity).reshape(rows, experts)
    lanes = -(-experts // 128) * 128
    weights = jnp.pad(weights, ((0, 0), (0, lanes - experts)))
    own_t, own_g, own_w, both_t, both_g = gather(
        layers, tokens.reshape(rows, width), out_grad.reshape(rows, width), weights
    )
    own_t = own_t.reshape(-1, width)
    own_g = own_g.reshape(-1, width)
    both_t = both_t.reshape(-1, width // 2)
    both_g = both_g.reshape(-1, width // 2)
    mine = jnp.arange(lanes, dtype=jnp.int32) == expert
    p = jnp.sum(jnp.where(mine, own_w.reshape(-1, lanes), 0.0), axis=1, keepdims=True)
    contract = (((1,), (1,)), ((), ()))
    rows_first = (((0,), (0,)), ((), ()))
    gate_pre = jnp.dot(own_t, w_gate, preferred_element_type=f32)
    up_pre = jnp.dot(own_t, w_up, preferred_element_type=f32)
    squash = jax.nn.sigmoid(gate_pre)
    active = gate_pre * squash
    hidden = (p * (active * up_pre)).astype(bf16)
    hidden_grad = p * jnp.dot(own_g, w_down, preferred_element_type=f32)
    gate_grad = (hidden_grad * up_pre * squash * (1.0 + gate_pre * (1.0 - squash))).astype(bf16)
    up_grad = (hidden_grad * active).astype(bf16)
    part_out = lax.dot_general(hidden, w_down, contract, preferred_element_type=f32).astype(bf16)
    part_dx = lax.dot_general(gate_grad, w_gate, contract, preferred_element_type=f32)
    part_dx = (part_dx + lax.dot_general(up_grad, w_up, contract, preferred_element_type=f32)).astype(bf16)
    moe, grad_in, *acts = give_back(
        layers, part_out.reshape(-1, rows, width), part_dx.reshape(-1, rows, width), (gate_grad, up_grad, hidden)
    )

    def outer(rows_in, act):
        return lax.dot_general(
            rows_in, act.reshape(-1, act.shape[2]), rows_first, preferred_element_type=f32
        )

    return (
        moe.reshape(tokens.shape),
        grad_in.reshape(tokens.shape),
        outer(both_t, acts[0]),
        outer(both_t, acts[1]),
        outer(both_g, acts[2]),
    )


def solution(mesh):
    return jax.shard_map(
        local,
        mesh=mesh,
        in_specs=(
            P(None, ("dp", "expert"), None),
            P(None, ("dp", "expert"), None),
            P(None, ("dp", "expert"), None),
            P(None, ("dp", "expert"), None),
            P(),
            P(None, "expert"),
            P(None, "expert"),
            P(None, "expert"),
        ),
        out_specs=(
            P(None, ("dp", "expert"), None),
            P(None, ("dp", "expert"), None),
            P("dp", "expert"),
            P("dp", "expert"),
            P("dp", "expert"),
        ),
        check_vma=False,
    )
```
